512 devices in a mesh: tile: 32 (over x, z_lo), beam: 16 (over y, z_hi, core).
Axes of the slice: x: 4, y: 4, z: 16 (z_hi: 2, z_lo: 8; z = z_hi * 8 + z_lo), core: 2. Of those that a mesh axis runs over, the one named last changes fastest.
Arguments:
- smatrix: bfloat16 [2, 2048, 512, 512], P(None, ('beam', 'tile')), may hold values from -6 to 6
- offset_y: int32 [512], replicated, may hold values from 0 to 511, as said below
- offset_x: int32 [512], replicated, may hold values from 0 to 511
- beam_qx: int32 [2048], P('beam'), may hold values from -64 to 63
- beam_qy: int32 [2048], P('beam'), may hold values from -64 to 63
- beam_amp: float32 [2048], P('beam'), may hold values from 0.5 to 2
- beam_phase: float32 [2048], P('beam'), may hold values from -3.140625 to 3.140625
Outputs:
- intensity: float32 [512, 128, 128], P(('tile', 'beam'))
The draws below stay inside these ranges and needn't reach their ends.
Inputs may be any that keep to these rules, and one draw needn't show every extreme that they name: `offset_y`: the window of position p starts in field rows 16 * (p // 16) to 16 * (p // 16) + 15.
All inputs are finite; a program needn't handle non-finite values.
Results may differ from the reference program's by a relative error of at most 0.017.
Values may be sent and summed in bfloat16 or wider, within the bound.
A program may use at most 128 MiB of HBM per device.

```python
import math
import jax
import jax.numpy as jnp
from jax import lax

BEAMS = 2048
CROP = 128
POS_DEV = 16
FIELD = 512
POSITIONS = 512
STRIP = 16
N_BEAM = 16


def draw_offset_y(key, part):
    places = jnp.arange(POSITIONS, dtype=jnp.int32)
    start = places // POS_DEV * STRIP
    jitter = jax.random.randint(key, (POSITIONS,), 0, STRIP, dtype=jnp.int32)
    slot = places % POS_DEV
    jitter = jnp.where(slot == 0, STRIP - 1, jnp.where(slot == 1, 0, jitter))
    return (start + jitter).astype(jnp.int32)


def with_ends(result, key, low, largest):
    shape = result.shape
    index_at = [jax.random.randint(jax.random.fold_in(key, axis), (), 0, shape[axis]) for axis in range(len(shape))]
    result = result.at[tuple(index_at)].set(low)
    longest = shape.index(max(shape))
    index_at[longest] = (index_at[longest] + 1) % shape[longest]
    return result.at[tuple(index_at)].set(largest)


def level_of(own_key, shape, pieces, smallest, top_value):
    loudness, own = 1.0, jax.random.fold_in(own_key, 6)
    for position, parts in pieces:
        draws = jnp.exp(jax.random.uniform(jax.random.fold_in(own, position), (parts,), jnp.float32, smallest / len(pieces), top_value / len(pieces)))
        loudness = loudness * jnp.repeat(draws, shape[position] // parts).reshape([-1 if axis == position else 1 for axis in range(len(shape))])
    return loudness


def normal_values(key, dims, spread, most, shards=(), held_as=jnp.bfloat16):
    drawn = spread * jax.random.normal(key, dims, jnp.float32)
    if shards:
        drawn = drawn * level_of(key, dims, shards, -0.22, 0.18)
    return jnp.clip(drawn, -most, most).astype(held_as)


def setup_inputs(seed: int = 0) -> dict:
    key_list = jax.random.split(jax.random.key(seed), 8)
    smatrix = normal_values(key_list[0], (2, BEAMS, FIELD, FIELD), 1.0, 6.0, ((1, 512),))
    offset_y = draw_offset_y(jax.random.fold_in(key_list[7], 71), 0)
    offset_x = with_ends(jax.random.randint(key_list[2], (POSITIONS,), 0, FIELD), jax.random.fold_in(key_list[2], 1), 0, FIELD - 1).astype(jnp.int32)
    beam_qx = with_ends(jax.random.randint(key_list[3], (BEAMS,), 0 - FIELD // 8, FIELD // 8), jax.random.fold_in(key_list[3], 1), 0 - FIELD // 8, (FIELD // 8) - 1).astype(jnp.int32)
    beam_qy = with_ends(jax.random.randint(key_list[4], (BEAMS,), 0 - FIELD // 8, FIELD // 8), jax.random.fold_in(key_list[4], 1), 0 - FIELD // 8, (FIELD // 8) - 1).astype(jnp.int32)
    beam_amp = jnp.clip(jnp.exp(math.log(2.0) - 1.3862944 * jax.random.uniform(key_list[5], (BEAMS,), jnp.float32) ** level_of(key_list[5], (BEAMS,), ((0, 16),), -0.2, 0.2)), 0.5, 2.0)
    beam_phase = jnp.clip(jax.random.uniform(key_list[6], (BEAMS,), jnp.float32, -3.140625, 3.140625), -3.140625, 3.140625)
    return {"smatrix": smatrix, "offset_y": offset_y, "offset_x": offset_x, "beam_qx": beam_qx, "beam_qy": beam_qy, "beam_amp": beam_amp, "beam_phase": beam_phase}


two_pi = 2.0 * math.pi

def reference(smatrix, offset_y, offset_x, beam_qx, beam_qy, beam_amp, beam_phase):
    group_beams = BEAMS // N_BEAM
    scale = beam_amp * (1.0 / math.sqrt(BEAMS))
    places = jnp.arange(CROP, dtype=jnp.int32)

    def one_position(pair):
        first_y, first_x = pair
        turns = ((first_x + CROP // 2) * beam_qx + (first_y + CROP // 2) * beam_qy) % FIELD
        angle = beam_phase - two_pi * turns.astype(jnp.float32) / FIELD
        w_real = lax.optimization_barrier((scale * jnp.cos(angle)).astype(jnp.bfloat16)).astype(jnp.float32)
        w_imag = lax.optimization_barrier((scale * jnp.sin(angle)).astype(jnp.bfloat16)).astype(jnp.float32)
        w_real = w_real.reshape(N_BEAM, group_beams)
        w_imag = w_imag.reshape(N_BEAM, group_beams)
        rows = ((first_y + places) % FIELD).astype(jnp.int32)
        cols = ((first_x + places) % FIELD).astype(jnp.int32)
        window = jnp.take(jnp.take(smatrix, rows, axis=2), cols, axis=3)
        window = window.astype(jnp.float32).reshape(2, N_BEAM, group_beams, CROP, CROP)
        part_re = jnp.einsum('gb,gbij->gij', w_real, window[0]) - jnp.einsum('gb,gbij->gij', w_imag, window[1])
        part_im = jnp.einsum('gb,gbij->gij', w_real, window[1]) + jnp.einsum('gb,gbij->gij', w_imag, window[0])
        part_re = lax.optimization_barrier(part_re.astype(jnp.bfloat16)).astype(jnp.float32)
        part_im = lax.optimization_barrier(part_im.astype(jnp.bfloat16)).astype(jnp.float32)
        exit_re = lax.optimization_barrier(jnp.sum(part_re, axis=0))
        exit_im = lax.optimization_barrier(jnp.sum(part_im, axis=0))
        spectrum = jnp.fft.fft2(exit_re + 1j * exit_im) / CROP
        return (spectrum.real * spectrum.real + spectrum.imag * spectrum.imag).astype(jnp.float32)
    return lax.map(one_position, (offset_y, offset_x))
```

```python
import math

import jax
import jax.numpy as jnp
from jax import lax
from jax.experimental import pallas as pl
from jax.experimental.pallas import tpu as pltpu
from jax.sharding import Mesh
from jax.sharding import PartitionSpec as P

CROP = 128
STRIP = 16
FIELD = 512
PLANES = 4
TILES = 8
STRIPS = 4
SOURCES = 8
DEPTH = 64

two_pi = 2.0 * math.pi


def mix_kernel(strips_ref, weight_ref, tile_ref, out_ref, wide, rows):
    def strip(r, carry):
        for k in range(PLANES):
            wide[k] = strips_ref[r, :, k * CROP : (k + 1) * CROP].astype(jnp.float32)

        def one_row(i, inner):
            field_row = jnp.concatenate(
                [wide[k, pl.ds(i, DEPTH, stride=STRIP), :].astype(jnp.bfloat16) for k in range(PLANES)], axis=1
            )
            full = jnp.dot(weight_ref[r], field_row, preferred_element_type=jnp.float32)
            place = tile_ref[r]
            picked = jnp.where(
                place < 2,
                jnp.where(place == 0, full[:, :128], full[:, 128:256]),
                jnp.where(place == 2, full[:, 256:384], full[:, 384:]),
            )
            rows[pl.ds(i, full.shape[0], stride=STRIP), :] = picked
            return inner

        lax.fori_loop(0, STRIP, one_row, 0)
        out_ref[r] = rows[...].astype(jnp.bfloat16)
        return carry

    lax.fori_loop(0, STRIPS, strip, 0)


def mix(strips, weights, tiles):
    count = weights.shape[1]
    return pl.pallas_call(
        mix_kernel,
        out_shape=jax.ShapeDtypeStruct((STRIPS, count * STRIP, CROP), jnp.bfloat16),
        in_specs=[pl.BlockSpec(memory_space=pltpu.VMEM)] * 3,
        out_specs=pl.BlockSpec(memory_space=pltpu.VMEM),
        scratch_shapes=[
            pltpu.VMEM((PLANES, DEPTH * STRIP, CROP), jnp.float32),
            pltpu.VMEM((count * STRIP, CROP), jnp.float32),
        ],
        compiler_params=pltpu.CompilerParams(vmem_limit_bytes=48 * 2**20),
    )(strips, weights, tiles)


def transform(exit_re, exit_im):
    places = jnp.arange(CROP, dtype=jnp.int32)
    ticks = places[:, None] * places[None, :] % CROP
    angle = two_pi * ticks.astype(jnp.float32) / CROP
    norm_factor = 1.0 / math.sqrt(CROP)
    table_re = jnp.cos(angle) * norm_factor
    table_im = -jnp.sin(angle) * norm_factor

    def dot(a, b):
        return jnp.dot(a, b, precision=lax.Precision.HIGHEST)

    half_re = dot(exit_re, table_re) - dot(exit_im, table_im)
    half_im = dot(exit_re, table_im) + dot(exit_im, table_re)
    full_re = dot(table_re, half_re) - dot(table_im, half_im)
    full_im = dot(table_re, half_im) + dot(table_im, half_re)
    return full_re * full_re + full_im * full_im


def per_strip(values, x, c):
    ny, nzh = values.shape[2:4]
    own = lax.dynamic_index_in_dim(values, x, 0, False)
    before = lax.dynamic_index_in_dim(values, (x + PLANES - 1) % PLANES, 0, False)
    s = STRIPS * c + jnp.arange(STRIPS)
    zl = jnp.arange(TILES)
    main = jnp.where((zl[None, :] <= s[:, None])[:, :, None, None, None], own[None], before[None])
    extra = lax.dynamic_slice_in_dim(before, STRIPS * c, STRIPS, 0)
    main = main.transpose(0, 2, 3, 1, 4).reshape(STRIPS, ny, nzh * TILES * 2)
    return jnp.concatenate([main, extra.reshape(STRIPS, ny, nzh * 2)], axis=2)


def local(smatrix, offset_y, offset_x, beam_qx, beam_qy, beam_amp, beam_phase):
    x, zl, c = (lax.axis_index(a) for a in ("x", "zl", "c"))
    y, zh = lax.axis_index("y"), lax.axis_index("zh")
    ny, nzh = lax.axis_size("y"), lax.axis_size("zh")
    nz = nzh * TILES
    beams = BEAMS_PER
    total = beam_qx.shape[0] * ny * nzh * 2

    params = jnp.stack([beam_qx.astype(jnp.float32), beam_qy.astype(jnp.float32), beam_amp, beam_phase])
    params = lax.dynamic_index_in_dim(params.reshape(4, PLANES, TILES, beams), zl, 2, False)
    params = lax.all_gather(params, "c", axis=2)
    params = jnp.broadcast_to(params[:, :, :, None, :], (4, PLANES, 2, 2, beams)).reshape(4, DEPTH)
    qx, qy = params[0].astype(jnp.int32), params[1].astype(jnp.int32)
    amp, phase = params[2] * (1.0 / math.sqrt(total)), params[3]
    part = jnp.arange(DEPTH) // beams % 2

    grid = (PLANES, TILES, ny, nzh, 2)
    first_y = per_strip(offset_y.reshape(grid), x, c)
    first_x = per_strip(offset_x.reshape(grid), x, c)
    turns = (first_x + CROP // 2)[..., None] * qx + (first_y + CROP // 2)[..., None] * qy
    quarter = (jnp.arange(2)[:, None] - part[None, :]) * (FIELD // 4)
    turns = (turns[..., None, :] + quarter) % FIELD
    weights = (amp * jnp.cos(phase - two_pi * turns.astype(jnp.float32) / FIELD)).astype(jnp.bfloat16)
    count = first_x.shape[1] * first_x.shape[2] * 2
    weights = weights.reshape(STRIPS, count, DEPTH)
    lanes = jnp.arange(CROP)
    tiles = (first_x[..., None] // CROP + (lanes < (first_x % CROP)[..., None])) % PLANES
    tiles = jnp.broadcast_to(tiles[..., None, :], (*first_x.shape, 2, CROP)).reshape(STRIPS, count, CROP)

    split = smatrix.reshape(2, beams, SOURCES, STRIPS, STRIP, FIELD)
    strips = lax.all_to_all(split, ("x", "c"), split_axis=2, concat_axis=0)
    strips = strips.transpose(3, 0, 1, 2, 4, 5).reshape(STRIPS, DEPTH * STRIP, FIELD)
    waves = mix(strips, weights, tiles)

    each = count // ny
    waves = waves.reshape(STRIPS, ny, each, STRIP, CROP)
    waves = lax.psum_scatter(waves, "y", scatter_dimension=1)
    main = waves[:, : nz * 4].reshape(STRIPS, nzh, TILES, 4, STRIP, CROP).transpose(1, 2, 0, 3, 4, 5)
    extra = waves[:, nz * 4 :].reshape(STRIPS, nzh, 4, STRIP, CROP).transpose(1, 0, 2, 3, 4)
    empty = jnp.zeros_like(extra)
    extra = jnp.where(c == 0, jnp.concatenate([extra, empty], 1), jnp.concatenate([empty, extra], 1))
    both = jnp.concatenate([main, extra[:, :, None]], axis=2).reshape(nz, STRIPS + 1, 4, STRIP, CROP)
    both = lax.psum_scatter(both, ("zh", "zl"), scatter_dimension=0).astype(jnp.float32)
    both = both.reshape(STRIPS + 1, 2, 2, STRIP, CROP).transpose(1, 0, 2, 3, 4)

    s = STRIPS * c + jnp.arange(STRIPS)
    flat = ((y * nzh + zh) * 2 + jnp.arange(2)).astype(jnp.int32)
    per_tile = ny * nzh * 2
    own_y = lax.dynamic_slice_in_dim(offset_y, (x * TILES + zl) * per_tile + flat[0], 2) % STRIP
    before_y = lax.dynamic_slice_in_dim(offset_y, (((x + PLANES - 1) % PLANES) * TILES + zl) * per_tile + flat[0], 2) % STRIP
    i = jnp.arange(STRIP)
    own_row = (s[None, :, None] * STRIP + i >= zl * STRIP + own_y[:, None, None])[:, :, None, :, None]
    own = jnp.where(own_row, both[:, :STRIPS], 0.0)
    below = (s < zl)[None, :, None, None, None]
    cut = (s == zl)[None, :, None, None, None] & (i < before_y[:, None])[:, None, None, :, None]
    before = jnp.where(below, both[:, :STRIPS], jnp.where(cut, both[:, STRIPS:], 0.0))

    def pick(pair, core):
        return lax.dynamic_index_in_dim(pair, core, 0, False)

    def sent(value, dx, flip):
        pairs = [
            (a * 2 + b, ((a - dx) % PLANES) * 2 + (b ^ flip)) for a in range(PLANES) for b in range(2)
        ]
        return lax.ppermute(value, ("x", "c"), pairs)

    same = pick(own, c) + sent(pick(before, c), 1, 0)
    other = sent(pick(own, 1 - c), 0, 1) + sent(pick(before, 1 - c), 1, 1)
    first, second = jnp.where(c == 0, same, other), jnp.where(c == 0, other, same)
    wave = jnp.concatenate([first, second], axis=0)
    wave = wave.transpose(1, 0, 2, 3).reshape(2, CROP, CROP)
    return transform(wave[0], wave[1])[None]


BEAMS_PER = 4


def solution(mesh):
    tile, beam = mesh.shape["tile"], mesh.shape["beam"]
    del tile
    shape = (PLANES, TILES, beam // 4 if beam >= 4 else 1, 2 if beam >= 4 else 1, 2)
    fine = Mesh(mesh.devices.reshape(shape), ("x", "zl", "y", "zh", "c"))
    group = ("y", "zh", "c")
    return jax.shard_map(
        local,
        mesh=fine,
        in_specs=(P(None, (*group, "x", "zl"), None, None), P(), P(), P(group), P(group), P(group), P(group)),
        out_specs=P(("x", "zl", *group), None, None),
        check_vma=False,
    )
```

```python
import functools
import math

import jax
import jax.numpy as jnp
import numpy as np
from jax import lax
from jax.experimental import pallas as pl
from jax.experimental.pallas import tpu as pltpu
from jax.sharding import Mesh
from jax.sharding import PartitionSpec as P

CROP = 128
STRIP = 16
FIELD = 512
PLANES = 4
TILES = 8
STRIPS = 4
SOURCES = 8
DEPTH = 64

two_pi = 2.0 * math.pi


def remote(source, target, send_sem, recv_sem, device):
    return pltpu.make_async_remote_copy(
        src_ref=source,
        dst_ref=target,
        send_sem=send_sem,
        recv_sem=recv_sem,
        device_id=device,
        device_id_type=pl.DeviceIdType.MESH,
    )


def loop(start, stop, body):
    def step(i, carry):
        body(i)
        return carry

    lax.fori_loop(start, stop, step, 0)


def probe_kernel(
    ny,
    nzh,
    smatrix,
    weight_ref,
    tile_ref,
    own_mask,
    cut_mask,
    dft,
    out_ref,
    raw,
    wide,
    rows,
    waves,
    ywave,
    summed,
    zwave,
    ewave,
    extra,
    own_part,
    low_part,
    last,
    full,
    local_sem,
    a_send,
    a_recv,
    y_send,
    y_recv,
    z_send,
    z_recv,
    e_send,
    e_recv,
    f_send,
    f_recv,
):
    x, zl, y, zh, c = (lax.axis_index(a) for a in ("x", "zl", "y", "zh", "c"))
    nz = nzh * TILES
    each = nz * 4 + nzh * 4
    z = zh * TILES + zl
    me = x * 2 + c
    before_x = lax.rem(x + PLANES - 1, PLANES)

    def peer(d):
        p = lax.rem(me + d, SOURCES)
        return p, {"x": p // 2, "c": lax.rem(p, 2)}

    def zpeer(d):
        p = lax.rem(z + d, nz)
        return p, {"zh": p // TILES, "zl": lax.rem(p, TILES)}

    def ypeer(d):
        p = lax.rem(y + d, ny)
        return p, {"y": p}

    def greet(peers, count):
        def one(d):
            pl.semaphore_signal(
                pltpu.get_barrier_semaphore(), inc=1, device_id=peers(d)[1], device_id_type=pl.DeviceIdType.MESH
            )

        loop(1, count, one)

    greet(peer, SOURCES)
    greet(ypeer, ny)
    greet(zpeer, nz)
    pl.semaphore_wait(pltpu.get_barrier_semaphore(), SOURCES + ny + nz - 3)

    def part_rows(p, r):
        return smatrix.at[:, pl.ds(pl.multiple_of(p * (STRIPS * STRIP) + r * STRIP, STRIP), STRIP), :]

    def raw_copy(d, r):
        p, device = peer(d)
        return remote(part_rows(p, r), raw.at[r, me], a_send.at[r, p], a_recv.at[r, me], device)

    def raw_own(r):
        return pltpu.make_async_copy(part_rows(me, r), raw.at[r, me], local_sem.at[r])

    def raw_start(r):
        loop(1, SOURCES, lambda d: raw_copy(d, r).start())
        raw_own(r).start()

    loop(0, STRIPS, raw_start)

    def raw_wait(d, r):
        p, device = peer(d)
        remote(raw.at[r, p], raw.at[r, p], a_send.at[r, p], a_recv.at[r, p], device).wait_recv()

    def y_copy(d, r):
        p, device = ypeer(d)
        return remote(waves.at[r, p], ywave.at[r, y], y_send.at[r, p], y_recv.at[r, y], device)

    def y_wait(d, r):
        p, device = ypeer(d)
        remote(ywave.at[r, p], ywave.at[r, p], y_send.at[r, p], y_recv.at[r, p], device).wait_recv()

    def z_copy(d, r):
        p, device = zpeer(d)
        return remote(summed.at[r, pl.ds(p * 4, 4)], zwave.at[r, z], z_send.at[r, p], z_recv.at[r, z], device)

    def z_wait(d, r):
        p, device = zpeer(d)
        remote(zwave.at[r, p], zwave.at[r, p], z_send.at[r, p], z_recv.at[r, p], device).wait_recv()

    def e_copy(h, r):
        return remote(
            summed.at[r, pl.ds((nz + h) * 4, 4)],
            ewave.at[z],
            e_send.at[r, h],
            e_recv.at[z],
            {"zh": h, "zl": c * STRIPS + r},
        )

    def e_each(r, act):
        def one(h):
            @pl.when(h * TILES + c * STRIPS + r != z)
            def _():
                act(e_copy(h, r))

        loop(0, nzh, one)

    def mixing(r):
        raw_own(r).wait()
        loop(1, SOURCES, lambda d: raw_wait(d, r))

        def widen(p):
            for k in range(PLANES):
                part = raw[r, p, :, :, k * CROP : (k + 1) * CROP].astype(jnp.float32)
                wide[k, pl.ds(pl.multiple_of(p * 128, 128), 128), :] = part.reshape(128, CROP)

        loop(0, SOURCES, widen)

        def one_row(i):
            field_row = jnp.concatenate(
                [wide[k, pl.ds(i, DEPTH, stride=STRIP), :].astype(jnp.bfloat16) for k in range(PLANES)], axis=1
            )
            product = jnp.dot(weight_ref[r], field_row, preferred_element_type=jnp.float32)
            place = tile_ref[r]
            picked = jnp.where(
                place < 2,
                jnp.where(place == 0, product[:, :128], product[:, 128:256]),
                jnp.where(place == 2, product[:, 256:384], product[:, 384:]),
            )
            rows[pl.ds(i, ny * each, stride=STRIP), :] = picked

        loop(0, STRIP, one_row)

        def narrow(p):
            size = each * STRIP
            part = rows[pl.ds(pl.multiple_of(p * size, STRIP), size), :].astype(jnp.bfloat16)
            waves[r, p] = part.reshape(each, STRIP, CROP)

        loop(0, ny, narrow)
        loop(1, ny, lambda d: y_copy(d, r).start())

    def summing(r):
        loop(1, ny, lambda d: y_wait(d, r))

        def block(b):
            at = pl.ds(b * 4, 4)
            total = waves[r, y, at].astype(jnp.float32)
            for d in range(1, ny):
                total += ywave[r, ypeer(d)[0], at].astype(jnp.float32)
            summed[r, at] = total.astype(jnp.bfloat16)

        loop(0, each // 4, block)
        loop(1, nz, lambda d: z_copy(d, r).start())
        e_each(r, lambda copy: copy.start())

    def stage(r):
        mixing(r)

        @pl.when(r > 0)
        def _():
            summing(r - 1)

    loop(0, STRIPS, stage)
    summing(STRIPS - 1)

    extra[...] = jnp.zeros_like(extra)

    @pl.when(zl // STRIPS == c)
    def _():
        def e_wait(d):
            p, device = zpeer(d)
            remote(ewave.at[p], ewave.at[p], e_send.at[0, 0], e_recv.at[p], device).wait_recv()

        loop(1, nz, e_wait)
        total = summed[lax.rem(zl, STRIPS), pl.ds((nz + zh) * 4, 4)].astype(jnp.float32)
        for d in range(1, nz):
            total += ewave[zpeer(d)[0]].astype(jnp.float32)
        extra[...] = total

    def closing(r):
        loop(1, nz, lambda d: z_wait(d, r))
        total = summed[r, pl.ds(z * 4, 4)].astype(jnp.float32)
        for d in range(1, nz):
            total += zwave[r, zpeer(d)[0]].astype(jnp.float32)
        s = c * STRIPS + r
        low = jnp.where(s < zl, 1.0, 0.0)
        cut = jnp.where(s == zl, 1.0, 0.0)
        for k in range(2):
            for part in range(2):
                value = total[2 * k + part]
                own_part[k, r, part] = value * own_mask[k, r]
                low_part[k, r, part] = value * low + extra[2 * k + part] * cut_mask[k] * cut

    loop(0, STRIPS, closing)

    other = 1 - c
    finals = [
        remote(own_part.at[other], last.at[0], f_send.at[0], f_recv.at[0], {"c": other}),
        remote(low_part.at[c], last.at[1], f_send.at[1], f_recv.at[1], {"x": before_x}),
        remote(low_part.at[other], last.at[2], f_send.at[2], f_recv.at[2], {"x": before_x, "c": other}),
    ]
    for copy in finals:
        copy.start()
    for copy in finals:
        copy.wait_recv()
    for r in range(STRIPS):
        for part in range(2):
            full[part, c * STRIPS + r] = own_part[c, r, part] + last[1, r, part]
            full[part, other * STRIPS + r] = last[0, r, part] + last[2, r, part]

    def dot(a, b):
        return jnp.dot(a, b, precision=lax.Precision.HIGHEST, preferred_element_type=jnp.float32)

    exit_re, exit_im = full[0].reshape(CROP, CROP), full[1].reshape(CROP, CROP)
    table_re, table_im = dft[0], dft[1]
    half_re = dot(exit_re, table_re) - dot(exit_im, table_im)
    half_im = dot(exit_re, table_im) + dot(exit_im, table_re)
    full_re = dot(table_re, half_re) - dot(table_im, half_im)
    full_im = dot(table_re, half_im) + dot(table_im, half_re)
    out_ref[...] = full_re * full_re + full_im * full_im

    for copy in finals:
        copy.wait_send()

    def sent(r):
        loop(1, SOURCES, lambda d: raw_copy(d, r).wait_send())
        loop(1, ny, lambda d: y_copy(d, r).wait_send())
        loop(1, nz, lambda d: z_copy(d, r).wait_send())
        e_each(r, lambda copy: copy.wait_send())

    loop(0, STRIPS, sent)


def probes(ny, nzh, smatrix, weights, tiles, own_mask, cut_mask, dft):
    nz = nzh * TILES
    each = nz * 4 + nzh * 4
    vmem = pl.BlockSpec(memory_space=pltpu.VMEM)
    half = jnp.bfloat16
    return pl.pallas_call(
        functools.partial(probe_kernel, ny, nzh),
        out_shape=jax.ShapeDtypeStruct((CROP, CROP), jnp.float32),
        in_specs=[pl.BlockSpec(memory_space=pl.ANY), vmem, vmem, vmem, vmem, vmem],
        out_specs=vmem,
        scratch_shapes=[
            pltpu.VMEM((STRIPS, SOURCES, 8, STRIP, FIELD), half),
            pltpu.VMEM((PLANES, DEPTH * STRIP, CROP), jnp.float32),
            pltpu.VMEM((ny * each * STRIP, CROP), jnp.float32),
            pltpu.VMEM((STRIPS, ny, each, STRIP, CROP), half),
            pltpu.VMEM((STRIPS, ny, each, STRIP, CROP), half),
            pltpu.VMEM((STRIPS, each, STRIP, CROP), half),
            pltpu.VMEM((STRIPS, nz, 4, STRIP, CROP), half),
            pltpu.VMEM((nz, 4, STRIP, CROP), half),
            pltpu.VMEM((4, STRIP, CROP), jnp.float32),
            pltpu.VMEM((2, STRIPS, 2, STRIP, CROP), jnp.float32),
            pltpu.VMEM((2, STRIPS, 2, STRIP, CROP), jnp.float32),
            pltpu.VMEM((3, STRIPS, 2, STRIP, CROP), jnp.float32),
            pltpu.VMEM((2, SOURCES, STRIP, CROP), jnp.float32),
            pltpu.SemaphoreType.DMA((STRIPS,)),
            pltpu.SemaphoreType.DMA((STRIPS, SOURCES)),
            pltpu.SemaphoreType.DMA((STRIPS, SOURCES)),
            pltpu.SemaphoreType.DMA((STRIPS, ny)),
            pltpu.SemaphoreType.DMA((STRIPS, ny)),
            pltpu.SemaphoreType.DMA((STRIPS, nz)),
            pltpu.SemaphoreType.DMA((STRIPS, nz)),
            pltpu.SemaphoreType.DMA((STRIPS, nzh)),
            pltpu.SemaphoreType.DMA((nz,)),
            pltpu.SemaphoreType.DMA((3,)),
            pltpu.SemaphoreType.DMA((3,)),
        ],
        compiler_params=pltpu.CompilerParams(
            collective_id=0, has_side_effects=True, vmem_limit_bytes=48 * 2**20
        ),
    )(smatrix, weights, tiles, own_mask, cut_mask, dft)


def dft_table():
    places = np.arange(CROP)
    angle = two_pi * (places[:, None] * places[None, :] % CROP) / CROP
    return np.stack([np.cos(angle), -np.sin(angle)]).astype(np.float32) / np.float32(math.sqrt(CROP))


def per_strip(values, x, c):
    ny, nzh = values.shape[2:4]
    own = lax.dynamic_index_in_dim(values, x, 0, False)
    before = lax.dynamic_index_in_dim(values, (x + PLANES - 1) % PLANES, 0, False)
    s = STRIPS * c + jnp.arange(STRIPS)
    zl = jnp.arange(TILES)
    main = jnp.where((zl[None, :] <= s[:, None])[:, :, None, None, None], own[None], before[None])
    extra = lax.dynamic_slice_in_dim(before, STRIPS * c, STRIPS, 0)
    main = main.transpose(0, 2, 3, 1, 4).reshape(STRIPS, ny, nzh * TILES * 2)
    return jnp.concatenate([main, extra.reshape(STRIPS, ny, nzh * 2)], axis=2)


def local(smatrix, offset_y, offset_x, beam_qx, beam_qy, beam_amp, beam_phase):
    x, zl, c = (lax.axis_index(a) for a in ("x", "zl", "c"))
    y, zh = lax.axis_index("y"), lax.axis_index("zh")
    ny, nzh = lax.axis_size("y"), lax.axis_size("zh")
    beams = BEAMS_PER
    total = beam_qx.shape[0] * ny * nzh * 2

    params = jnp.stack([beam_qx.astype(jnp.float32), beam_qy.astype(jnp.float32), beam_amp, beam_phase])
    params = lax.dynamic_index_in_dim(params.reshape(4, PLANES, TILES, beams), zl, 2, False)
    params = lax.all_gather(params, "c", axis=2)
    params = jnp.broadcast_to(params[:, :, :, None, :], (4, PLANES, 2, 2, beams)).reshape(4, DEPTH)
    qx, qy = params[0].astype(jnp.int32), params[1].astype(jnp.int32)
    amp, phase = params[2] * (1.0 / math.sqrt(total)), params[3]
    part = jnp.arange(DEPTH) // beams % 2

    grid = (PLANES, TILES, ny, nzh, 2)
    first_y = per_strip(offset_y.reshape(grid), x, c)
    first_x = per_strip(offset_x.reshape(grid), x, c)
    turns = (first_x + CROP // 2)[..., None] * qx + (first_y + CROP // 2)[..., None] * qy
    quarter = (jnp.arange(2)[:, None] - part[None, :]) * (FIELD // 4)
    turns = (turns[..., None, :] + quarter) % FIELD
    weights = (amp * jnp.cos(phase - two_pi * turns.astype(jnp.float32) / FIELD)).astype(jnp.bfloat16)
    count = first_x.shape[1] * first_x.shape[2] * 2
    weights = weights.reshape(STRIPS, count, DEPTH)
    lanes = jnp.arange(CROP)
    tiles = (first_x[..., None] // CROP + (lanes < (first_x % CROP)[..., None])) % PLANES
    tiles = jnp.broadcast_to(tiles[..., None, :], (*first_x.shape, 2, CROP)).reshape(STRIPS, count, CROP)

    s = STRIPS * c + jnp.arange(STRIPS)
    first = (y * nzh + zh) * 2
    per_tile = ny * nzh * 2
    own_y = lax.dynamic_slice_in_dim(offset_y, (x * TILES + zl) * per_tile + first, 2) % STRIP
    before_x = (x + PLANES - 1) % PLANES
    before_y = lax.dynamic_slice_in_dim(offset_y, (before_x * TILES + zl) * per_tile + first, 2) % STRIP
    i = jnp.arange(STRIP)
    own_mask = s[None, :, None] * STRIP + i >= zl * STRIP + own_y[:, None, None]
    own_mask = jnp.broadcast_to(own_mask[..., None].astype(jnp.float32), (2, STRIPS, STRIP, CROP))
    cut_mask = i < before_y[:, None]
    cut_mask = jnp.broadcast_to(cut_mask[..., None].astype(jnp.float32), (2, STRIP, CROP))
    smatrix = smatrix.reshape(2 * beams, FIELD, FIELD)
    return probes(ny, nzh, smatrix, weights, tiles, own_mask, cut_mask, jnp.asarray(dft_table()))[None]


BEAMS_PER = 4


def solution(mesh):
    tile, beam = mesh.shape["tile"], mesh.shape["beam"]
    del tile
    shape = (PLANES, TILES, beam // 4 if beam >= 4 else 1, 2 if beam >= 4 else 1, 2)
    fine = Mesh(mesh.devices.reshape(shape), ("x", "zl", "y", "zh", "c"))
    group = ("y", "zh", "c")
    return jax.shard_map(
        local,
        mesh=fine,
        in_specs=(P(None, (*group, "x", "zl"), None, None), P(), P(), P(group), P(group), P(group), P(group)),
        out_specs=P(("x", "zl", *group), None, None),
        check_vma=False,
    )
```

```python
import functools
import math

import jax
import jax.numpy as jnp
import numpy as np
from jax import lax
from jax.experimental import pallas as pl
from jax.experimental.pallas import tpu as pltpu
from jax.sharding import Mesh
from jax.sharding import PartitionSpec as P

CROP = 128
STRIP = 16
FIELD = 512
PLANES = 4
TILES = 8
STRIPS = 4
SOURCES = 8
QUAD = 4
BEAMS_PER = 4
UNROLL = 4
DEPTH = 64

two_pi = 2.0 * math.pi


def remote(source, target, send_sem, recv_sem, device):
    return pltpu.make_async_remote_copy(
        src_ref=source,
        dst_ref=target,
        send_sem=send_sem,
        recv_sem=recv_sem,
        device_id=device,
        device_id_type=pl.DeviceIdType.MESH,
    )


def loop(start, stop, body):
    def step(i, carry):
        body(i)
        return carry

    lax.fori_loop(start, stop, step, 0)


def dft_table():
    places = np.arange(CROP)
    angle = two_pi * (places[:, None] * places[None, :] % CROP) / CROP
    return np.stack([np.cos(angle), -np.sin(angle)]).astype(np.float32) / np.float32(math.sqrt(CROP))


def probe_kernel(
    ny,
    nzh,
    smatrix,
    offset_y_ref,
    offset_x_ref,
    beam_qx_ref,
    beam_qy_ref,
    beam_amp_ref,
    beam_phase_ref,
    dft_ref,
    out_ref,
    offset_y,
    offset_x,
    beam_qx,
    beam_qy,
    beam_amp,
    beam_phase,
    raw,
    wide,
    rows,
    waves,
    ywave,
    relay,
    main1,
    extra1,
    zmain1,
    zextra1,
    main2,
    extra2,
    zmain2,
    zextra2,
    own_part,
    low_part,
    last,
    full,
    params,
    weight_own,
    weight_low,
    weight,
    tile_own,
    tile_low,
    tile,
    dft,
    local_sem,
    small_sem,
    a_send,
    a_recv,
    y_send,
    y_recv,
    z_send,
    z_recv,
    e_send,
    e_recv,
    f_send,
    f_recv,
    p_send,
    p_recv,
):
    x, zl, y, zh, c = (lax.axis_index(a) for a in ("x", "zl", "y", "zh", "c"))
    pair = nzh * 2
    per_tile = ny * pair
    per_plane = TILES * per_tile
    count = per_plane + per_tile
    each = (TILES + 1) * pair
    nq = nzh * 2
    half = zl // QUAD
    q, p = zh * 2 + half, lax.rem(zl, QUAD)
    me = x * 2 + c
    before_x = lax.rem(x + PLANES - 1, PLANES)
    other = 1 - c

    def peer(d):
        k = lax.rem(me + d, SOURCES)
        return k, {"x": k // 2, "c": lax.rem(k, 2)}

    def ypeer(d):
        k = lax.rem(y + d, ny)
        return k, {"y": k}

    def ppeer(d):
        k = lax.rem(p + d, QUAD)
        return k, {"zl": half * QUAD + k}

    def qpeer(d):
        k = lax.rem(q + d, nq)
        return k, {"zh": k // 2, "zl": lax.rem(k, 2) * QUAD + p}

    def greet(peers, number):
        def one(d):
            pl.semaphore_signal(
                pltpu.get_barrier_semaphore(), inc=1, device_id=peers(d)[1], device_id_type=pl.DeviceIdType.MESH
            )

        loop(1, number, one)

    beam_copies = [
        pltpu.make_async_copy(source, target, small_sem.at[j])
        for j, (source, target) in enumerate(
            (
                (beam_qx_ref, beam_qx),
                (beam_qy_ref, beam_qy),
                (beam_amp_ref, beam_amp),
                (beam_phase_ref, beam_phase),
            )
        )
    ]
    offset_copies = [
        pltpu.make_async_copy(offset_y_ref, offset_y, small_sem.at[4]),
        pltpu.make_async_copy(offset_x_ref, offset_x, small_sem.at[5]),
    ]
    dft_copy = pltpu.make_async_copy(dft_ref, dft, small_sem.at[6])
    for copy in (*beam_copies, *offset_copies, dft_copy):
        copy.start()
    greet(peer, SOURCES)
    for d in (1, ny - 1) if ny > 1 else ():
        pl.semaphore_signal(
            pltpu.get_barrier_semaphore(), inc=1, device_id=ypeer(d)[1], device_id_type=pl.DeviceIdType.MESH
        )
    greet(ppeer, QUAD)
    greet(qpeer, nq)
    pl.semaphore_wait(pltpu.get_barrier_semaphore(), SOURCES + min(ny - 1, 2) + QUAD + nq - 3)

    def part_rows(k, r):
        at = pl.ds(pl.multiple_of(k * (STRIPS * STRIP) + r * STRIP, STRIP), STRIP)
        return smatrix.at[:, :, at, :]

    def raw_copy(d, r):
        k, device = peer(d)
        return remote(part_rows(k, r), raw.at[r, me], a_send.at[r, k], a_recv.at[r, me], device)

    def raw_own(r):
        return pltpu.make_async_copy(part_rows(me, r), raw.at[r, me], local_sem.at[r])

    def raw_start(r):
        loop(1, SOURCES, lambda d: raw_copy(d, r).start())
        raw_own(r).start()

    for copy in beam_copies:
        copy.wait()
    params[0] = jnp.zeros((8, 128), jnp.float32)
    params[0, 0:1, :] = beam_qx[...].astype(jnp.float32).reshape(1, 128)
    params[0, 1:2, :] = beam_qy[...].astype(jnp.float32).reshape(1, 128)
    params[0, 2:3, :] = beam_amp[...].reshape(1, 128)
    params[0, 3:4, :] = beam_phase[...].reshape(1, 128)
    param_copy = remote(params.at[0], params.at[1], p_send, p_recv, {"c": other})
    param_copy.start()
    loop(0, STRIPS, raw_start)
    for copy in offset_copies:
        copy.wait()

    term = lax.broadcasted_iota(jnp.int32, (DEPTH, 128), 0)
    lane = lax.broadcasted_iota(jnp.int32, (DEPTH, 128), 1)
    hot = lane == ((term // 16) * TILES + zl) * BEAMS_PER + term % BEAMS_PER
    part = term[:, :1] // BEAMS_PER % 2
    param_copy.wait_recv()

    def column(j):
        mine, theirs = params[0, j : j + 1, :], params[1, j : j + 1, :]
        both = jnp.where(term // 8 % 2 == c, mine, theirs)
        return jnp.sum(jnp.where(hot, both, 0.0), axis=1, keepdims=True)

    qx, qy = column(0).astype(jnp.int32), column(1).astype(jnp.int32)
    amp = column(2) * (1.0 / math.sqrt(ny * nzh * 2 * 128))
    phase = column(3)

    def plane_values(ref, plane):
        return ref[pl.ds(pl.multiple_of(plane * per_plane, per_plane), per_plane)].reshape(1, per_plane)

    for plane, to_weight, to_tile in ((x, weight_own, tile_own), (before_x, weight_low, tile_low)):
        first_y, first_x = plane_values(offset_y, plane), plane_values(offset_x, plane)
        turns = (first_x + CROP // 2) * qx + (first_y + CROP // 2) * qy
        for k in range(2):
            turned = (turns + (k - part) * (FIELD // 4)) & (FIELD - 1)
            value = amp * jnp.cos(phase - turned.astype(jnp.float32) * (two_pi / FIELD))
            to_weight[k] = value.T
        column_lane = lax.broadcasted_iota(jnp.int32, (CROP, per_plane), 0)
        place = (first_x // CROP + jnp.where(column_lane < (first_x & (CROP - 1)), 1, 0)) & (PLANES - 1)
        to_tile[...] = place.T

    def raw_wait(d, r):
        k, device = peer(d)
        remote(raw.at[r, k], raw.at[r, k], a_send.at[r, k], a_recv.at[r, k], device).wait_recv()

    cut = each // 2
    far = ypeer(2)[0]

    def y_near(d, r, k):
        t, device = ypeer(1 if d == 0 else ny - 1)
        at = pl.ds(cut, cut) if d == 0 else pl.ds(0, cut)
        return remote(
            waves.at[r, k, t, at], ywave.at[r, k, d, at], y_send.at[r, k, d], y_recv.at[r, k, d], device
        )

    def y_far(d, r, k):
        device = ypeer(1 if d == 0 else ny - 1)[1]
        at = pl.ds(0, cut) if d == 0 else pl.ds(cut, cut)
        return remote(
            waves.at[r, k, far, at], relay.at[r, k, d], y_send.at[r, k, 2 + d], y_recv.at[r, k, 2 + d], device
        )

    def y_last(d, r, k):
        t, device = ypeer(1 if d == 0 else ny - 1)
        at = pl.ds(0, cut) if d == 0 else pl.ds(cut, cut)
        return remote(
            waves.at[r, k, t, at], ywave.at[r, k, d, at], y_send.at[r, k, 4 + d], y_recv.at[r, k, 4 + d], device
        )

    def y_start(r, k):
        if ny > 1:
            for make in (y_far, y_near):
                for d in range(2):
                    make(d, r, k).start()

    def y_relay(r, k):
        if ny > 1:
            for d in range(2):
                y_far(d, r, k).wait_recv()
                t = ypeer(1 if d == 0 else ny - 1)[0]
                at = pl.ds(0, cut) if d == 0 else pl.ds(cut, cut)
                value = waves[r, k, t, at].astype(jnp.float32) + relay[r, k, d].astype(jnp.float32)
                waves[r, k, t, at] = value.astype(jnp.bfloat16)
                y_last(d, r, k).start()

    def y_done(r, k):
        if ny > 1:
            for make in (y_far, y_near, y_last):
                for d in range(2):
                    make(d, r, k).wait_send()

    def z1_copy(d, r, k):
        t, device = ppeer(d)
        return remote(main1.at[r, k, :, t], zmain1.at[r, k, p], z_send.at[0, r, k, t], z_recv.at[0, r, k, p], device)

    def z1_wait(d, r, k):
        t, device = ppeer(d)
        remote(
            zmain1.at[r, k, t], zmain1.at[r, k, t], z_send.at[0, r, k, t], z_recv.at[0, r, k, t], device
        ).wait_recv()

    def e1_copy(r, k):
        return remote(
            extra1.at[r, k], zextra1.at[k, p], e_send.at[0, r, k], e_recv.at[0, k, p], {"zl": half * QUAD + r}
        )

    def e1_wait(d, k):
        t, device = ppeer(d)
        remote(zextra1.at[k, t], zextra1.at[k, t], e_send.at[0, 0, k], e_recv.at[0, k, t], device).wait_recv()

    def z2_copy(d, r, k):
        t, device = qpeer(d)
        return remote(
            main2.at[r, k, lax.rem(t, 2), pl.ds(t // 2 * 2, 2)],
            zmain2.at[r, k, q],
            z_send.at[1, r, k, t],
            z_recv.at[1, r, k, q],
            device,
        )

    def z2_wait(d, r, k):
        t, device = qpeer(d)
        remote(
            zmain2.at[r, k, t], zmain2.at[r, k, t], z_send.at[1, r, k, t], z_recv.at[1, r, k, t], device
        ).wait_recv()

    def e2_copy(h, k):
        return remote(
            extra2.at[k, pl.ds(h * 2, 2)],
            zextra2.at[k, q],
            e_send.at[1, h, k],
            e_recv.at[1, k, q],
            {"zh": h, "zl": c * QUAD + p},
        )

    def e2_each(k, act):
        def one(h):
            @pl.when(h * 2 + c != q)
            def _():
                act(e2_copy(h, k))

        loop(0, nzh, one)

    def e2_wait(d, k):
        t, device = qpeer(d)
        remote(zextra2.at[k, t], zextra2.at[k, t], e_send.at[1, 0, k], e_recv.at[1, k, t], device).wait_recv()

    def mixing(r):
        s = c * STRIPS + r
        tile_of = lax.broadcasted_iota(jnp.int32, (per_plane, DEPTH), 0) // per_tile
        place_of = lax.broadcasted_iota(jnp.int32, (per_plane, CROP), 0) // per_tile
        crossing = pl.ds(pl.multiple_of(s * per_tile, per_tile), per_tile)
        for k in range(2):
            start = k * count
            main = jnp.where(tile_of <= s, weight_own[k], weight_low[k])
            weight[start : start + per_plane] = main.astype(jnp.bfloat16)
            weight[start + per_plane : start + count] = weight_low[k, crossing].astype(jnp.bfloat16)
        tile[:per_plane] = jnp.where(place_of <= s, tile_own[...], tile_low[...])
        tile[per_plane:] = tile_low[crossing]
        raw_own(r).wait()
        loop(1, SOURCES, lambda d: raw_wait(d, r))

        def widen(b):
            for k in range(PLANES):
                block = raw[r, b, :, :, :, k * CROP : (k + 1) * CROP].astype(jnp.float32)
                wide[k, pl.ds(pl.multiple_of(b * 128, 128), 128), :] = block.reshape(128, CROP)

        loop(0, SOURCES, widen)

        def one_row(i):
            field_row = jnp.concatenate(
                [wide[k, pl.ds(i, DEPTH, stride=STRIP), :].astype(jnp.bfloat16) for k in range(PLANES)], axis=1
            )
            product = jnp.dot(weight[...], field_row, preferred_element_type=jnp.float32)
            place = tile[...]
            for k in range(2):
                here = product[k * count : (k + 1) * count]
                picked = jnp.where(
                    place < 2,
                    jnp.where(place == 0, here[:, :128], here[:, 128:256]),
                    jnp.where(place == 2, here[:, 256:384], here[:, 384:]),
                )
                rows[k, pl.ds(i, count, stride=STRIP), :] = picked

        def some_rows(i):
            for j in range(UNROLL):
                one_row(i * UNROLL + j)

        loop(0, STRIP // UNROLL, some_rows)

        for k in range(2):

            def narrow(j):
                size = pair * STRIP
                block = rows[k, pl.ds(pl.multiple_of(j * size, STRIP), size), :].astype(jnp.bfloat16)
                waves[r, k, lax.rem(j, ny), pl.ds(j // ny * pair, pair)] = block.reshape(pair, STRIP, CROP)

            loop(0, (TILES + 1) * ny, narrow)
            y_start(r, k)

    def y_sum(r, k):
        if ny > 1:
            for d in range(2):
                y_near(d, r, k).wait_recv()
                y_last(d, r, k).wait_recv()

        def total(g):
            at = pl.ds(g * pair, pair)
            value = waves[r, k, y, at].astype(jnp.float32)
            for d in range(min(ny - 1, 2)):
                value += ywave[r, k, d, at].astype(jnp.float32)
            return value.astype(jnp.bfloat16)

        def block(g):
            main1[r, k, g // QUAD, lax.rem(g, QUAD)] = total(g)

        loop(0, TILES, block)
        extra1[r, k] = total(TILES)
        loop(1, QUAD, lambda d: z1_copy(d, r, k).start())

        @pl.when(p != r)
        def _():
            e1_copy(r, k).start()

    def z1_sum(r, k):
        loop(1, QUAD, lambda d: z1_wait(d, r, k))
        for a in range(2):
            value = main1[r, k, a, p].astype(jnp.float32)
            for d in range(1, QUAD):
                value += zmain1[r, k, ppeer(d)[0], a].astype(jnp.float32)
            main2[r, k, a] = value.astype(jnp.bfloat16)
        loop(1, nq, lambda d: z2_copy(d, r, k).start())

        @pl.when(p == r)
        def _():
            loop(1, QUAD, lambda d: e1_wait(d, k))
            value = extra1[r, k].astype(jnp.float32)
            for d in range(1, QUAD):
                value += zextra1[k, ppeer(d)[0]].astype(jnp.float32)
            extra2[k] = value.astype(jnp.bfloat16)
            e2_each(k, lambda copy: copy.start())

    def stage(r):
        @pl.when(r > 0)
        def _():
            y_sum(r - 1, 0)

        @pl.when(r > 1)
        def _():
            z1_sum(r - 2, 1)

        mixing(r)

        @pl.when(r > 0)
        def _():
            y_sum(r - 1, 1)
            z1_sum(r - 1, 0)

        y_relay(r, 0)
        y_relay(r, 1)

    loop(0, STRIPS, stage)
    spot = lax.broadcasted_iota(jnp.int32, (1, per_plane), 1)
    row = lax.broadcasted_iota(jnp.int32, (STRIP, CROP), 0)
    mine = zl * per_tile + (y * nzh + zh) * 2

    def first_row(plane, k):
        picked = jnp.where(spot == mine + k, plane_values(offset_y, plane) & (STRIP - 1), 0)
        return jnp.sum(picked.astype(jnp.float32), axis=1, keepdims=True).astype(jnp.int32)

    own_rows = [row >= first_row(x, k) for k in range(2)]
    cut_rows = [row < first_row(before_x, k) for k in range(2)]

    def final_copies(r):
        return [
            remote(own_part.at[other, r], last.at[0, r], f_send.at[0, r], f_recv.at[0, r], {"c": other}),
            remote(low_part.at[c, r], last.at[1, r], f_send.at[1, r], f_recv.at[1, r], {"x": before_x}),
            remote(low_part.at[other, r], last.at[2, r], f_send.at[2, r], f_recv.at[2, r], {"x": before_x, "c": other}),
        ]

    def closing(r):
        s = c * STRIPS + r
        own = jnp.where(s > zl, 1.0, 0.0)
        low = jnp.where(s < zl, 1.0, 0.0)
        edge = jnp.where(s == zl, 1.0, 0.0)
        for k in range(2):
            loop(1, nq, lambda d: z2_wait(d, r, k))
            value = main2[r, k, half, pl.ds(zh * 2, 2)].astype(jnp.float32)
            for d in range(1, nq):
                value += zmain2[r, k, qpeer(d)[0]].astype(jnp.float32)
            for j in range(2):
                own_part[j, r, k] = value[j] * (own + jnp.where(own_rows[j], edge, 0.0))
                low_part[j, r, k] = value[j] * low

        @pl.when(s == zl)
        def _():
            for k in range(2):
                loop(1, nq, lambda d: e2_wait(d, k))
                value = extra2[k, pl.ds(zh * 2, 2)].astype(jnp.float32)
                for d in range(1, nq):
                    value += zextra2[k, qpeer(d)[0]].astype(jnp.float32)
                for j in range(2):
                    low_part[j, r, k] = jnp.where(cut_rows[j], value[j], 0.0)

        for copy in final_copies(r):
            copy.start()

    def dot(a, b):
        return jnp.dot(a, b, precision=lax.Precision.HIGHEST, preferred_element_type=jnp.float32)

    def finish(r):
        for copy in final_copies(r):
            copy.wait_recv()
        exits = [own_part[c, r, k] + last[1, r, k] for k in range(2)]
        exits += [last[0, r, k] + last[2, r, k] for k in range(2)]
        lines = dot(jnp.concatenate(exits, axis=0), jnp.concatenate([dft[0], dft[1]], axis=1))
        for core, k in ((c, 0), (other, 2)):
            real, imag = lines[k * STRIP : (k + 1) * STRIP], lines[(k + 1) * STRIP : (k + 2) * STRIP]
            full[core * STRIPS + r, :, :CROP] = real[:, :CROP] - imag[:, CROP:]
            full[core * STRIPS + r, :, CROP:] = real[:, CROP:] + imag[:, :CROP]

    z1_sum(STRIPS - 2, 1)
    y_sum(STRIPS - 1, 0)
    dft_copy.wait()
    loop(0, STRIPS - 2, closing)
    y_sum(STRIPS - 1, 1)
    closing(STRIPS - 2)
    z1_sum(STRIPS - 1, 0)
    z1_sum(STRIPS - 1, 1)

    def sent(r):
        loop(1, SOURCES, lambda d: raw_copy(d, r).wait_send())
        for k in range(2):
            y_done(r, k)
            loop(1, QUAD, lambda d: z1_copy(d, r, k).wait_send())
            loop(1, nq, lambda d: z2_copy(d, r, k).wait_send())

            @pl.when(p != r)
            def _():
                e1_copy(r, k).wait_send()

            @pl.when(p == r)
            def _():
                e2_each(k, lambda copy: copy.wait_send())

    loop(0, STRIPS - 1, finish)
    closing(STRIPS - 1)
    loop(0, STRIPS, sent)
    param_copy.wait_send()
    finish(STRIPS - 1)
    spectrum = dot(jnp.concatenate([dft[0], dft[1]], axis=0), full[...].reshape(CROP, 2 * CROP))
    full_re = spectrum[:CROP, :CROP] - spectrum[CROP:, CROP:]
    full_im = spectrum[:CROP, CROP:] + spectrum[CROP:, :CROP]
    out_ref[0] = full_re * full_re + full_im * full_im

    def final_sent(r):
        for copy in final_copies(r):
            copy.wait_send()

    loop(0, STRIPS, final_sent)


def local(smatrix, offset_y, offset_x, beam_qx, beam_qy, beam_amp, beam_phase):
    ny, nzh = lax.axis_size("y"), lax.axis_size("zh")
    pair = nzh * 2
    per_plane = TILES * ny * pair
    count = per_plane + ny * pair
    each = (TILES + 1) * pair
    nq = nzh * 2
    vmem = pl.BlockSpec(memory_space=pltpu.VMEM)
    hbm = pl.BlockSpec(memory_space=pltpu.HBM)
    bf16, f32 = jnp.bfloat16, jnp.float32

    def blocks(kind, *lead):
        return pltpu.VMEM((*lead, STRIP, CROP), kind)

    dma = pltpu.SemaphoreType.DMA
    return pl.pallas_call(
        functools.partial(probe_kernel, ny, nzh),
        out_shape=jax.ShapeDtypeStruct((1, CROP, CROP), f32),
        in_specs=[hbm] * 8,
        out_specs=vmem,
        scratch_shapes=[
            pltpu.VMEM(offset_y.shape, jnp.int32),
            pltpu.VMEM(offset_x.shape, jnp.int32),
            pltpu.VMEM(beam_qx.shape, jnp.int32),
            pltpu.VMEM(beam_qy.shape, jnp.int32),
            pltpu.VMEM(beam_amp.shape, f32),
            pltpu.VMEM(beam_phase.shape, f32),
            pltpu.VMEM((STRIPS, SOURCES, 2, BEAMS_PER, STRIP, FIELD), bf16),
            pltpu.VMEM((PLANES, DEPTH * STRIP, CROP), f32),
            pltpu.VMEM((2, count * STRIP, CROP), f32),
            blocks(bf16, STRIPS, 2, ny, each),
            blocks(bf16, STRIPS, 2, 2, each),
            blocks(bf16, STRIPS, 2, 2, each // 2),
            blocks(bf16, STRIPS, 2, 2, QUAD, pair),
            blocks(bf16, STRIPS, 2, pair),
            blocks(bf16, STRIPS, 2, QUAD, 2, pair),
            blocks(bf16, 2, QUAD, pair),
            blocks(bf16, STRIPS, 2, 2, pair),
            blocks(bf16, 2, pair),
            blocks(bf16, STRIPS, 2, nq, 2),
            blocks(bf16, 2, nq, 2),
            blocks(f32, 2, STRIPS, 2),
            blocks(f32, 2, STRIPS, 2),
            blocks(f32, 3, STRIPS, 2),
            pltpu.VMEM((SOURCES, STRIP, 2 * CROP), f32),
            pltpu.VMEM((2, 8, 128), f32),
            pltpu.VMEM((2, per_plane, DEPTH), f32),
            pltpu.VMEM((2, per_plane, DEPTH), f32),
            pltpu.VMEM((2 * count, DEPTH), bf16),
            pltpu.VMEM((per_plane, CROP), jnp.int32),
            pltpu.VMEM((per_plane, CROP), jnp.int32),
            pltpu.VMEM((count, CROP), jnp.int32),
            pltpu.VMEM((2, CROP, CROP), f32),
            dma((STRIPS,)),
            dma((7,)),
            dma((STRIPS, SOURCES)),
            dma((STRIPS, SOURCES)),
            dma((STRIPS, 2, 6)),
            dma((STRIPS, 2, 6)),
            dma((2, STRIPS, 2, QUAD)),
            dma((2, STRIPS, 2, QUAD)),
            dma((2, STRIPS, 2)),
            dma((2, 2, QUAD)),
            dma((3, STRIPS)),
            dma((3, STRIPS)),
            dma,
            dma,
        ],
        compiler_params=pltpu.CompilerParams(
            collective_id=0, has_side_effects=True, vmem_limit_bytes=60 * 2**20
        ),
    )(smatrix, offset_y, offset_x, beam_qx, beam_qy, beam_amp, beam_phase, jnp.asarray(dft_table()))


def solution(mesh):
    tile, beam = mesh.shape["tile"], mesh.shape["beam"]
    del tile
    shape = (PLANES, TILES, beam // 4 if beam >= 4 else 1, 2 if beam >= 4 else 1, 2)
    fine = Mesh(mesh.devices.reshape(shape), ("x", "zl", "y", "zh", "c"))
    group = ("y", "zh", "c")
    return jax.shard_map(
        local,
        mesh=fine,
        in_specs=(P(None, (*group, "x", "zl"), None, None), P(), P(), P(group), P(group), P(group), P(group)),
        out_specs=P(("x", "zl", *group), None, None),
        check_vma=False,
    )
```

```python
import functools
import math

import jax
import jax.numpy as jnp
import numpy as np
from jax import lax
from jax.experimental import pallas as pl
from jax.experimental.pallas import tpu as pltpu
from jax.sharding import Mesh
from jax.sharding import PartitionSpec as P

CROP = 128
STRIP = 16
FIELD = 512
PLANES = 4
TILES = 8
STRIPS = 4
SOURCES = 8
QUAD = 4
BEAMS_PER = 4
UNROLL = 8
DEPTH = 64

two_pi = 2.0 * math.pi


def remote(source, target, send_sem, recv_sem, device):
    return pltpu.make_async_remote_copy(
        src_ref=source,
        dst_ref=target,
        send_sem=send_sem,
        recv_sem=recv_sem,
        device_id=device,
        device_id_type=pl.DeviceIdType.MESH,
    )


def loop(start, stop, body):
    def step(i, carry):
        body(i)
        return carry

    lax.fori_loop(start, stop, step, 0)


def dft_table():
    places = np.arange(CROP)
    angle = two_pi * (places[:, None] * places[None, :] % CROP) / CROP
    return np.stack([np.cos(angle), -np.sin(angle)]).astype(np.float32) / np.float32(math.sqrt(CROP))


def probe_kernel(
    ny,
    nzh,
    smatrix,
    offset_y_ref,
    offset_x_ref,
    beam_qx_ref,
    beam_qy_ref,
    beam_amp_ref,
    beam_phase_ref,
    dft_ref,
    out_ref,
    offset_y,
    offset_x,
    beam_qx,
    beam_qy,
    beam_amp,
    beam_phase,
    raw,
    wide,
    rows,
    waves,
    ywave,
    relay,
    main1,
    extra1,
    zmain1,
    zextra1,
    main2,
    extra2,
    zmain2,
    zextra2,
    own_part,
    low_part,
    last,
    full,
    params,
    weight_own,
    weight_low,
    weight,
    tile_own,
    tile_low,
    tile,
    dft,
    local_sem,
    small_sem,
    a_send,
    a_recv,
    y_send,
    y_recv,
    z_send,
    z_recv,
    e_send,
    e_recv,
    f_send,
    f_recv,
    p_send,
    p_recv,
):
    x, zl, y, zh, c = (lax.axis_index(a) for a in ("x", "zl", "y", "zh", "c"))
    pair = nzh * 2
    per_tile = ny * pair
    per_plane = TILES * per_tile
    count = per_plane + per_tile
    each = (TILES + 1) * pair
    nq = nzh * 2
    half = zl // QUAD
    q, p = zh * 2 + half, lax.rem(zl, QUAD)
    me = x * 2 + c
    before_x = lax.rem(x + PLANES - 1, PLANES)
    other = 1 - c

    def peer(d):
        k = lax.rem(me + d, SOURCES)
        return k, {"x": k // 2, "c": lax.rem(k, 2)}

    def ypeer(d):
        k = lax.rem(y + d, ny)
        return k, {"y": k}

    def ppeer(d):
        k = lax.rem(p + d, QUAD)
        return k, {"zl": half * QUAD + k}

    def qpeer(d):
        k = lax.rem(q + d, nq)
        return k, {"zh": k // 2, "zl": lax.rem(k, 2) * QUAD + p}

    def greet(peers, number):
        def one(d):
            pl.semaphore_signal(
                pltpu.get_barrier_semaphore(), inc=1, device_id=peers(d)[1], device_id_type=pl.DeviceIdType.MESH
            )

        loop(1, number, one)

    beam_copies = [
        pltpu.make_async_copy(source, target, small_sem.at[j])
        for j, (source, target) in enumerate(
            (
                (beam_qx_ref, beam_qx),
                (beam_qy_ref, beam_qy),
                (beam_amp_ref, beam_amp),
                (beam_phase_ref, beam_phase),
            )
        )
    ]
    offset_copies = [
        pltpu.make_async_copy(offset_y_ref, offset_y, small_sem.at[4]),
        pltpu.make_async_copy(offset_x_ref, offset_x, small_sem.at[5]),
    ]
    dft_copy = pltpu.make_async_copy(dft_ref, dft, small_sem.at[6])
    for copy in (*beam_copies, *offset_copies, dft_copy):
        copy.start()
    greet(peer, SOURCES)
    for d in (1, ny - 1) if ny > 1 else ():
        pl.semaphore_signal(
            pltpu.get_barrier_semaphore(), inc=1, device_id=ypeer(d)[1], device_id_type=pl.DeviceIdType.MESH
        )
    greet(ppeer, QUAD)
    greet(qpeer, nq)
    pl.semaphore_wait(pltpu.get_barrier_semaphore(), SOURCES + min(ny - 1, 2) + QUAD + nq - 3)

    def part_rows(k, r):
        at = pl.ds(pl.multiple_of(k * (STRIPS * STRIP) + r * STRIP, STRIP), STRIP)
        return smatrix.at[:, :, at, :]

    def raw_copy(d, r):
        k, device = peer(d)
        return remote(part_rows(k, r), raw.at[r, me], a_send.at[r, k], a_recv.at[r, me], device)

    def raw_own(r):
        return pltpu.make_async_copy(part_rows(me, r), raw.at[r, me], local_sem.at[r])

    def raw_start(r):
        loop(1, SOURCES, lambda d: raw_copy(d, r).start())
        raw_own(r).start()

    for copy in beam_copies:
        copy.wait()
    params[0] = jnp.zeros((8, 128), jnp.float32)
    params[0, 0:1, :] = beam_qx[...].astype(jnp.float32).reshape(1, 128)
    params[0, 1:2, :] = beam_qy[...].astype(jnp.float32).reshape(1, 128)
    params[0, 2:3, :] = beam_amp[...].reshape(1, 128)
    params[0, 3:4, :] = beam_phase[...].reshape(1, 128)
    param_copy = remote(params.at[0], params.at[1], p_send, p_recv, {"c": other})
    param_copy.start()
    loop(0, STRIPS, raw_start)
    for copy in offset_copies:
        copy.wait()

    term = lax.broadcasted_iota(jnp.int32, (DEPTH, 128), 0)
    lane = lax.broadcasted_iota(jnp.int32, (DEPTH, 128), 1)
    hot = lane == ((term // 16) * TILES + zl) * BEAMS_PER + term % BEAMS_PER
    part = term[:, :1] // BEAMS_PER % 2
    param_copy.wait_recv()

    def column(j):
        mine, theirs = params[0, j : j + 1, :], params[1, j : j + 1, :]
        both = jnp.where(term // 8 % 2 == c, mine, theirs)
        return jnp.sum(jnp.where(hot, both, 0.0), axis=1, keepdims=True)

    qx, qy = column(0).astype(jnp.int32), column(1).astype(jnp.int32)
    amp = column(2) * (1.0 / math.sqrt(ny * nzh * 2 * 128))
    phase = column(3)

    def plane_values(ref, plane):
        return ref[pl.ds(pl.multiple_of(plane * per_plane, per_plane), per_plane)].reshape(1, per_plane)

    for plane, to_weight, to_tile in ((x, weight_own, tile_own), (before_x, weight_low, tile_low)):
        first_y, first_x = plane_values(offset_y, plane), plane_values(offset_x, plane)
        turns = (first_x + CROP // 2) * qx + (first_y + CROP // 2) * qy
        for k in range(2):
            turned = (turns + (k - part) * (FIELD // 4)) & (FIELD - 1)
            value = amp * jnp.cos(phase - turned.astype(jnp.float32) * (two_pi / FIELD))
            to_weight[k] = value.T
        column_lane = lax.broadcasted_iota(jnp.int32, (CROP, per_plane), 0)
        place = (first_x // CROP + jnp.where(column_lane < (first_x & (CROP - 1)), 1, 0)) & (PLANES - 1)
        to_tile[...] = place.T

    def raw_wait(d, r):
        k, device = peer(d)
        remote(raw.at[r, k], raw.at[r, k], a_send.at[r, k], a_recv.at[r, k], device).wait_recv()

    cut = each // 2
    far = ypeer(2)[0]

    def y_near(d, r, k):
        t, device = ypeer(1 if d == 0 else ny - 1)
        at = pl.ds(cut, cut) if d == 0 else pl.ds(0, cut)
        return remote(
            waves.at[r, k, t, at], ywave.at[r, k, d, at], y_send.at[r, k, d], y_recv.at[r, k, d], device
        )

    def y_far(d, r, k):
        device = ypeer(1 if d == 0 else ny - 1)[1]
        at = pl.ds(0, cut) if d == 0 else pl.ds(cut, cut)
        return remote(
            waves.at[r, k, far, at], relay.at[r, k, d], y_send.at[r, k, 2 + d], y_recv.at[r, k, 2 + d], device
        )

    def y_last(d, r, k):
        t, device = ypeer(1 if d == 0 else ny - 1)
        at = pl.ds(0, cut) if d == 0 else pl.ds(cut, cut)
        return remote(
            waves.at[r, k, t, at], ywave.at[r, k, d, at], y_send.at[r, k, 4 + d], y_recv.at[r, k, 4 + d], device
        )

    def y_start(r, k):
        if ny > 1:
            for make in (y_far, y_near):
                for d in range(2):
                    make(d, r, k).start()

    def y_relay(r, k):
        if ny > 1:
            for d in range(2):
                y_far(d, r, k).wait_recv()
                t = ypeer(1 if d == 0 else ny - 1)[0]
                at = pl.ds(0, cut) if d == 0 else pl.ds(cut, cut)
                value = waves[r, k, t, at].astype(jnp.float32) + relay[r, k, d].astype(jnp.float32)
                waves[r, k, t, at] = value.astype(jnp.bfloat16)
                y_last(d, r, k).start()

    def y_done(r, k):
        if ny > 1:
            for make in (y_far, y_near, y_last):
                for d in range(2):
                    make(d, r, k).wait_send()

    def z1_copy(d, r, k):
        t, device = ppeer(d)
        return remote(main1.at[r, k, :, t], zmain1.at[r, k, p], z_send.at[0, r, k, t], z_recv.at[0, r, k, p], device)

    def z1_wait(d, r, k):
        t, device = ppeer(d)
        remote(
            zmain1.at[r, k, t], zmain1.at[r, k, t], z_send.at[0, r, k, t], z_recv.at[0, r, k, t], device
        ).wait_recv()

    def e1_copy(r, k):
        return remote(
            extra1.at[r, k], zextra1.at[k, p], e_send.at[0, r, k], e_recv.at[0, k, p], {"zl": half * QUAD + r}
        )

    def e1_wait(d, k):
        t, device = ppeer(d)
        remote(zextra1.at[k, t], zextra1.at[k, t], e_send.at[0, 0, k], e_recv.at[0, k, t], device).wait_recv()

    def z2_copy(d, r, k):
        t, device = qpeer(d)
        return remote(
            main2.at[r, k, lax.rem(t, 2), pl.ds(t // 2 * 2, 2)],
            zmain2.at[r, k, q],
            z_send.at[1, r, k, t],
            z_recv.at[1, r, k, q],
            device,
        )

    def z2_wait(d, r, k):
        t, device = qpeer(d)
        remote(
            zmain2.at[r, k, t], zmain2.at[r, k, t], z_send.at[1, r, k, t], z_recv.at[1, r, k, t], device
        ).wait_recv()

    def e2_copy(h, k):
        return remote(
            extra2.at[k, pl.ds(h * 2, 2)],
            zextra2.at[k, q],
            e_send.at[1, h, k],
            e_recv.at[1, k, q],
            {"zh": h, "zl": c * QUAD + p},
        )

    def e2_each(k, act):
        def one(h):
            @pl.when(h * 2 + c != q)
            def _():
                act(e2_copy(h, k))

        loop(0, nzh, one)

    def e2_wait(d, k):
        t, device = qpeer(d)
        remote(zextra2.at[k, t], zextra2.at[k, t], e_send.at[1, 0, k], e_recv.at[1, k, t], device).wait_recv()

    def mixing(r):
        s = c * STRIPS + r
        tile_of = lax.broadcasted_iota(jnp.int32, (per_plane, DEPTH), 0) // per_tile
        place_of = lax.broadcasted_iota(jnp.int32, (per_plane, CROP), 0) // per_tile
        crossing = pl.ds(pl.multiple_of(s * per_tile, per_tile), per_tile)
        for k in range(2):
            start = k * count
            main = jnp.where(tile_of <= s, weight_own[k], weight_low[k])
            weight[start : start + per_plane] = main.astype(jnp.bfloat16)
            weight[start + per_plane : start + count] = weight_low[k, crossing].astype(jnp.bfloat16)
        tile[:per_plane] = jnp.where(place_of <= s, tile_own[...], tile_low[...])
        tile[per_plane:] = tile_low[crossing]
        raw_own(r).wait()
        loop(1, SOURCES, lambda d: raw_wait(d, r))

        def widen(b):
            for k in range(PLANES):
                block = raw[r, b, :, :, :, k * CROP : (k + 1) * CROP].astype(jnp.float32)
                wide[k, pl.ds(pl.multiple_of(b * 128, 128), 128), :] = block.reshape(128, CROP)

        loop(0, SOURCES, widen)

        def one_row(i, k):
            field_row = jnp.concatenate(
                [wide[t, pl.ds(i, DEPTH, stride=STRIP), :].astype(jnp.bfloat16) for t in range(PLANES)], axis=1
            )
            here = jnp.dot(weight[k * count : (k + 1) * count], field_row, preferred_element_type=jnp.float32)
            place = tile[...]
            picked = jnp.where(
                place < 2,
                jnp.where(place == 0, here[:, :128], here[:, 128:256]),
                jnp.where(place == 2, here[:, 256:384], here[:, 384:]),
            )
            rows[k, pl.ds(i, count, stride=STRIP), :] = picked

        for k in range(2):

            def some_rows(i):
                for j in range(UNROLL):
                    one_row(i * UNROLL + j, k)

            loop(0, STRIP // UNROLL, some_rows)

            def narrow(j):
                size = pair * STRIP
                block = rows[k, pl.ds(pl.multiple_of(j * size, STRIP), size), :].astype(jnp.bfloat16)
                waves[r, k, lax.rem(j, ny), pl.ds(j // ny * pair, pair)] = block.reshape(pair, STRIP, CROP)

            loop(0, (TILES + 1) * ny, narrow)
            y_start(r, k)

    def y_sum(r, k):
        if ny > 1:
            for d in range(2):
                y_near(d, r, k).wait_recv()
                y_last(d, r, k).wait_recv()

        def total(g):
            at = pl.ds(g * pair, pair)
            value = waves[r, k, y, at].astype(jnp.float32)
            for d in range(min(ny - 1, 2)):
                value += ywave[r, k, d, at].astype(jnp.float32)
            return value.astype(jnp.bfloat16)

        def block(g):
            main1[r, k, g // QUAD, lax.rem(g, QUAD)] = total(g)

        loop(0, TILES, block)
        extra1[r, k] = total(TILES)
        loop(1, QUAD, lambda d: z1_copy(d, r, k).start())

        @pl.when(p != r)
        def _():
            e1_copy(r, k).start()

    def z1_sum(r, k):
        loop(1, QUAD, lambda d: z1_wait(d, r, k))
        for a in range(2):
            value = main1[r, k, a, p].astype(jnp.float32)
            for d in range(1, QUAD):
                value += zmain1[r, k, ppeer(d)[0], a].astype(jnp.float32)
            main2[r, k, a] = value.astype(jnp.bfloat16)
        loop(1, nq, lambda d: z2_copy(d, r, k).start())

        @pl.when(p == r)
        def _():
            loop(1, QUAD, lambda d: e1_wait(d, k))
            value = extra1[r, k].astype(jnp.float32)
            for d in range(1, QUAD):
                value += zextra1[k, ppeer(d)[0]].astype(jnp.float32)
            extra2[k] = value.astype(jnp.bfloat16)
            e2_each(k, lambda copy: copy.start())

    def stage(r):
        @pl.when(r > 0)
        def _():
            y_sum(r - 1, 0)

        @pl.when(r > 1)
        def _():
            z1_sum(r - 2, 1)

        mixing(r)
        y_relay(r, 0)

        @pl.when(r > 0)
        def _():
            y_sum(r - 1, 1)
            z1_sum(r - 1, 0)

        y_relay(r, 1)

    loop(0, STRIPS, stage)
    spot = lax.broadcasted_iota(jnp.int32, (1, per_plane), 1)
    row = lax.broadcasted_iota(jnp.int32, (STRIP, CROP), 0)
    mine = zl * per_tile + (y * nzh + zh) * 2

    def first_row(plane, k):
        picked = jnp.where(spot == mine + k, plane_values(offset_y, plane) & (STRIP - 1), 0)
        return jnp.sum(picked.astype(jnp.float32), axis=1, keepdims=True).astype(jnp.int32)

    own_rows = [row >= first_row(x, k) for k in range(2)]
    cut_rows = [row < first_row(before_x, k) for k in range(2)]

    def final_copies(r):
        return [
            remote(own_part.at[other, r], last.at[0, r], f_send.at[0, r], f_recv.at[0, r], {"c": other}),
            remote(low_part.at[c, r], last.at[1, r], f_send.at[1, r], f_recv.at[1, r], {"x": before_x}),
            remote(low_part.at[other, r], last.at[2, r], f_send.at[2, r], f_recv.at[2, r], {"x": before_x, "c": other}),
        ]

    def closing(r):
        s = c * STRIPS + r
        own = jnp.where(s > zl, 1.0, 0.0)
        low = jnp.where(s < zl, 1.0, 0.0)
        edge = jnp.where(s == zl, 1.0, 0.0)
        for k in range(2):
            loop(1, nq, lambda d: z2_wait(d, r, k))
            value = main2[r, k, half, pl.ds(zh * 2, 2)].astype(jnp.float32)
            for d in range(1, nq):
                value += zmain2[r, k, qpeer(d)[0]].astype(jnp.float32)
            for j in range(2):
                own_part[j, r, k] = value[j] * (own + jnp.where(own_rows[j], edge, 0.0))
                low_part[j, r, k] = value[j] * low

        @pl.when(s == zl)
        def _():
            for k in range(2):
                loop(1, nq, lambda d: e2_wait(d, k))
                value = extra2[k, pl.ds(zh * 2, 2)].astype(jnp.float32)
                for d in range(1, nq):
                    value += zextra2[k, qpeer(d)[0]].astype(jnp.float32)
                for j in range(2):
                    low_part[j, r, k] = jnp.where(cut_rows[j], value[j], 0.0)

        for copy in final_copies(r):
            copy.start()

    def dot(a, b):
        return jnp.dot(a, b, precision=lax.Precision.HIGHEST, preferred_element_type=jnp.float32)

    def finish(r):
        for copy in final_copies(r):
            copy.wait_recv()
        exits = [own_part[c, r, k] + last[1, r, k] for k in range(2)]
        exits += [last[0, r, k] + last[2, r, k] for k in range(2)]
        lines = dot(jnp.concatenate(exits, axis=0), jnp.concatenate([dft[0], dft[1]], axis=1))
        for core, k in ((c, 0), (other, 2)):
            real, imag = lines[k * STRIP : (k + 1) * STRIP], lines[(k + 1) * STRIP : (k + 2) * STRIP]
            full[core * STRIPS + r, :, :CROP] = real[:, :CROP] - imag[:, CROP:]
            full[core * STRIPS + r, :, CROP:] = real[:, CROP:] + imag[:, :CROP]

    z1_sum(STRIPS - 2, 1)
    y_sum(STRIPS - 1, 0)
    dft_copy.wait()
    loop(0, STRIPS - 2, closing)
    y_sum(STRIPS - 1, 1)
    closing(STRIPS - 2)
    z1_sum(STRIPS - 1, 0)
    z1_sum(STRIPS - 1, 1)

    def sent(r):
        loop(1, SOURCES, lambda d: raw_copy(d, r).wait_send())
        for k in range(2):
            y_done(r, k)
            loop(1, QUAD, lambda d: z1_copy(d, r, k).wait_send())
            loop(1, nq, lambda d: z2_copy(d, r, k).wait_send())

            @pl.when(p != r)
            def _():
                e1_copy(r, k).wait_send()

            @pl.when(p == r)
            def _():
                e2_each(k, lambda copy: copy.wait_send())

    loop(0, STRIPS - 1, finish)
    loop(0, STRIPS, sent)
    param_copy.wait_send()
    closing(STRIPS - 1)
    finish(STRIPS - 1)
    spectrum = dot(jnp.concatenate([dft[0], dft[1]], axis=0), full[...].reshape(CROP, 2 * CROP))
    full_re = spectrum[:CROP, :CROP] - spectrum[CROP:, CROP:]
    full_im = spectrum[:CROP, CROP:] + spectrum[CROP:, :CROP]
    out_ref[0] = full_re * full_re + full_im * full_im

    def final_sent(r):
        for copy in final_copies(r):
            copy.wait_send()

    loop(0, STRIPS, final_sent)


def local(smatrix, offset_y, offset_x, beam_qx, beam_qy, beam_amp, beam_phase):
    ny, nzh = lax.axis_size("y"), lax.axis_size("zh")
    pair = nzh * 2
    per_plane = TILES * ny * pair
    count = per_plane + ny * pair
    each = (TILES + 1) * pair
    nq = nzh * 2
    vmem = pl.BlockSpec(memory_space=pltpu.VMEM)
    hbm = pl.BlockSpec(memory_space=pltpu.HBM)
    bf16, f32 = jnp.bfloat16, jnp.float32

    def blocks(kind, *lead):
        return pltpu.VMEM((*lead, STRIP, CROP), kind)

    dma = pltpu.SemaphoreType.DMA
    return pl.pallas_call(
        functools.partial(probe_kernel, ny, nzh),
        out_shape=jax.ShapeDtypeStruct((1, CROP, CROP), f32),
        in_specs=[hbm] * 8,
        out_specs=vmem,
        scratch_shapes=[
            pltpu.VMEM(offset_y.shape, jnp.int32),
            pltpu.VMEM(offset_x.shape, jnp.int32),
            pltpu.VMEM(beam_qx.shape, jnp.int32),
            pltpu.VMEM(beam_qy.shape, jnp.int32),
            pltpu.VMEM(beam_amp.shape, f32),
            pltpu.VMEM(beam_phase.shape, f32),
            pltpu.VMEM((STRIPS, SOURCES, 2, BEAMS_PER, STRIP, FIELD), bf16),
            pltpu.VMEM((PLANES, DEPTH * STRIP, CROP), f32),
            pltpu.VMEM((2, count * STRIP, CROP), f32),
            blocks(bf16, STRIPS, 2, ny, each),
            blocks(bf16, STRIPS, 2, 2, each),
            blocks(bf16, STRIPS, 2, 2, each // 2),
            blocks(bf16, STRIPS, 2, 2, QUAD, pair),
            blocks(bf16, STRIPS, 2, pair),
            blocks(bf16, STRIPS, 2, QUAD, 2, pair),
            blocks(bf16, 2, QUAD, pair),
            blocks(bf16, STRIPS, 2, 2, pair),
            blocks(bf16, 2, pair),
            blocks(bf16, STRIPS, 2, nq, 2),
            blocks(bf16, 2, nq, 2),
            blocks(f32, 2, STRIPS, 2),
            blocks(f32, 2, STRIPS, 2),
            blocks(f32, 3, STRIPS, 2),
            pltpu.VMEM((SOURCES, STRIP, 2 * CROP), f32),
            pltpu.VMEM((2, 8, 128), f32),
            pltpu.VMEM((2, per_plane, DEPTH), f32),
            pltpu.VMEM((2, per_plane, DEPTH), f32),
            pltpu.VMEM((2 * count, DEPTH), bf16),
            pltpu.VMEM((per_plane, CROP), jnp.int32),
            pltpu.VMEM((per_plane, CROP), jnp.int32),
            pltpu.VMEM((count, CROP), jnp.int32),
            pltpu.VMEM((2, CROP, CROP), f32),
            dma((STRIPS,)),
            dma((7,)),
            dma((STRIPS, SOURCES)),
            dma((STRIPS, SOURCES)),
            dma((STRIPS, 2, 6)),
            dma((STRIPS, 2, 6)),
            dma((2, STRIPS, 2, QUAD)),
            dma((2, STRIPS, 2, QUAD)),
            dma((2, STRIPS, 2)),
            dma((2, 2, QUAD)),
            dma((3, STRIPS)),
            dma((3, STRIPS)),
            dma,
            dma,
        ],
        compiler_params=pltpu.CompilerParams(
            collective_id=0, has_side_effects=True, vmem_limit_bytes=60 * 2**20
        ),
    )(smatrix, offset_y, offset_x, beam_qx, beam_qy, beam_amp, beam_phase, jnp.asarray(dft_table()))


def solution(mesh):
    tile, beam = mesh.shape["tile"], mesh.shape["beam"]
    del tile
    shape = (PLANES, TILES, beam // 4 if beam >= 4 else 1, 2 if beam >= 4 else 1, 2)
    fine = Mesh(mesh.devices.reshape(shape), ("x", "zl", "y", "zh", "c"))
    group = ("y", "zh", "c")
    return jax.shard_map(
        local,
        mesh=fine,
        in_specs=(P(None, (*group, "x", "zl"), None, None), P(), P(), P(group), P(group), P(group), P(group)),
        out_specs=P(("x", "zl", *group), None, None),
        check_vma=False,
    )
```
